512 devices in a mesh: row: 32 (over z, x_hi, core), col: 16 (over x_lo, y).
Axes of the slice: x: 4 (x_hi: 2, x_lo: 2; x = x_hi * 2 + x_lo), y: 8, z: 8, core: 2. Of those that a mesh axis runs over, the one named last changes fastest.
Arguments:
- leg_table: bfloat16 [900, 12288], P(None, ('row', 'col')), may hold values from -5 to 5
- coef_code: int32 [12288], replicated, may hold values from 2 to 601
- colat_idx: int32 [6144], replicated, may hold values from 0 to 899
- lon_idx: int32 [6144], replicated, may hold values from 0 to 3599
- gap_mask: int32 [6144], replicated, may hold values 0 or 1
- obs_weight: float32 [6144], replicated, may hold values from 0.1 to 10
- gradient: float32 [6144], replicated, may hold values from -6 to 6
Outputs:
- normal: float32 [16, 12288, 768], P('col', 'row')
- rhs: float32 [12288], P('row')
The draws below stay inside these ranges and needn't reach their ends.
Inputs may be any that keep to these rules, and one draw needn't show every extreme that they name: coef_code[c] // 2 is the coefficient's order m and coef_code[c] % 2 is 0 for a cosine and 1 for a sine term.
All inputs are finite; a program needn't handle non-finite values.
Results may differ from the reference program's by a relative error of at most 0.0044.
Values may be sent and summed in bfloat16 or wider, within the bound.
A program may use at most 64 MiB of HBM per device.

```python
import math
import jax
import jax.numpy as jnp
from jax import lax

NC = 12288
MMAX = 300
NTHETA = 900
NLON = 3600
OBS = 6144
SUB = 24
N_ROW = 32
N_COL = 16


def touch_ends(array, rng, smallest, high):
    index_at = [jax.random.randint(jax.random.fold_in(rng, axis), (), 0, length) for axis, length in enumerate(array.shape)]
    main_axis = array.shape.index(max(array.shape))
    beside = index_at[:main_axis] + [(index_at[main_axis] + 1) % array.shape[main_axis]] + index_at[main_axis + 1:]
    return array.at[tuple(index_at)].set(smallest).at[tuple(beside)].set(high)


def levels(rng, dims, shards, low, high):
    gain = 1.0
    for axis_at, blocks in shards:
        draws = jax.random.uniform(jax.random.fold_in(jax.random.fold_in(rng, 6), axis_at), (blocks,), jnp.float32, low / len(shards), high / len(shards))
        gain = gain * jnp.repeat(jnp.exp(draws), dims[axis_at] // blocks).reshape((-1,) + (1,) * (len(dims) - 1 - axis_at))
    return gain


def normal_values(rng, shape, deviation, reach, cuts=(), held_as=jnp.bfloat16):
    values = jax.random.normal(rng, shape, jnp.float32) * deviation
    if len(cuts) > 0:
        values = levels(rng, shape, cuts, -0.22, 0.18) * values
    return jnp.clip(values, min=-reach, max=reach).astype(held_as)


def setup_inputs(seed: int = 0) -> dict:
    key_list = jax.random.split(jax.random.key(seed), 8)
    leg_table = normal_values(key_list[0], (NTHETA, NC), 1.0, 5.0, ((1, 512),))
    coef_code = touch_ends(jax.random.randint(key_list[1], (NC,), 2, 2 * MMAX + 2), jax.random.fold_in(key_list[1], 1), 2, (2 * MMAX + 2) - 1).astype(jnp.int32)
    colat_idx = touch_ends(jax.random.randint(key_list[2], (OBS,), 0, NTHETA), jax.random.fold_in(key_list[2], 1), 0, NTHETA - 1).astype(jnp.int32)
    lon_idx = touch_ends(jax.random.randint(key_list[3], (OBS,), 0, NLON), jax.random.fold_in(key_list[3], 1), 0, NLON - 1).astype(jnp.int32)
    gap_mask = touch_ends((jax.random.randint(key_list[4], (OBS,), 0, 8) < 7).astype(jnp.int32), jax.random.fold_in(key_list[4], 1), 0, 1)
    obs_weight = jnp.clip(jnp.exp(jax.random.uniform(key_list[5], (OBS,), jnp.float32, math.log(0.1), math.log(10.0))), 0.1, 10.0)
    gradient = normal_values(key_list[6], (OBS,), 1.0, 6.0, (), jnp.float32)
    return {"leg_table": leg_table, "coef_code": coef_code, "colat_idx": colat_idx, "lon_idx": lon_idx, "gap_mask": gap_mask, "obs_weight": obs_weight, "gradient": gradient}


def synthesize(table, codes, colat_idx, lon_idx):
    rows = jnp.take(table, colat_idx, axis=0).astype(jnp.float32)
    order = codes // 2
    kind = (codes % 2).astype(jnp.float32)
    phase = (lon_idx[:, None] * order[None, :]) % NLON
    angle = phase.astype(jnp.float32) * (2.0 * math.pi / NLON) - kind[None, :] * (0.5 * math.pi)
    return (rows * jnp.cos(angle)).astype(jnp.bfloat16)


def reference(leg_table, coef_code, colat_idx, lon_idx, gap_mask, obs_weight, gradient):
    scales = obs_weight * gap_mask.astype(jnp.float32)
    design = synthesize(leg_table, coef_code, colat_idx, lon_idx)
    left = (design.astype(jnp.float32) * scales[:, None]).astype(jnp.bfloat16)
    weighted = (scales * gradient).astype(jnp.bfloat16)
    rhs = jnp.dot(weighted, design, preferred_element_type=jnp.float32) / OBS
    blocks = design.reshape(OBS, N_ROW, N_COL, SUB).transpose(2, 0, 1, 3)
    left_t = left.T

    def one_block(block):
        return jnp.dot(left_t, block.reshape(OBS, N_ROW * SUB), preferred_element_type=jnp.float32) / OBS

    normal = lax.map(one_block, blocks)
    return normal, rhs
```

```python
import functools

import jax
import jax.numpy as jnp
from jax import lax
from jax.experimental import pallas as pl
from jax.experimental.pallas import tpu as pltpu
from jax.sharding import PartitionSpec as P

NLON = 3600
NTHETA = 900
OBS = 6144
SUB = 24
HALF = OBS // 2
BLOCK = 768
N_BLOCK = HALF // BLOCK
TILE = 384
F32 = jnp.float32
BF16 = jnp.bfloat16
MESH = pl.DeviceIdType.MESH
N_SEND = 66


def sin_turns(w):
    s = w * w
    p = -76.58128455924857 + s * 39.76072207493176
    p = 81.60248074286099 + s * p
    p = -41.341680668063056 + s * p
    p = 6.283185280261415 + s * p
    return w * p


def cos_turns(f):
    return sin_turns(0.25 - jnp.abs(f - jnp.round(f)))


def turns(x):
    return (x - NLON * jnp.round(x * (1.0 / NLON))) * (1.0 / NLON)


def dot(a, b, ca, cb, precision=None):
    return lax.dot_general(
        a, b, (((ca,), (cb,)), ((), ())), preferred_element_type=F32, precision=precision
    )


def kernel(
    leg_ref, code_ref, mask_ref, weight_ref, grad_ref, colat_ref, lon_ref,
    own_ref, rhs_ref, far_ref, far_rhs_ref,
    slots, fold, table, trig, cos_b, sin_b, codes, gathered, s_wide, g_wide,
    total, part, rhs_acc, rhs_part, send_sem, slot_sem, far_sem,
):
    row, col = lax.axis_index("row"), lax.axis_index("col")
    z, h, c = row // 4, (row // 2) % 2, row % 2
    p, y = col // 8, col % 8

    def rid(z_, h_, c_):
        return z_ * 4 + h_ * 2 + c_

    def cid(p_, y_):
        return p_ * 8 + y_

    sib = (rid(z, h, 1 - c), col)
    over_p = (row, cid(1 - p, y))
    over_h = (rid(z, 1 - h, c), col)
    y_up, y_down = (row, cid(p, (y + 1) % 8)), (row, cid(p, (y + 7) % 8))
    z_up, z_down = (rid((z + 1) % 8, h, c), col), (rid((z + 7) % 8, h, c), col)
    peers = (sib, over_p, over_h, y_up, y_down, z_up, z_down)

    barrier = pltpu.get_barrier_semaphore()
    for peer in peers:
        pl.semaphore_signal(barrier, inc=1, device_id=peer, device_id_type=MESH)

    def row_slot(core, plane, y_):
        return core * 16 + plane * 8 + y_

    def col_slot(z_, plane, core):
        return 32 + z_ * 4 + plane * 2 + core

    fold[...] = jnp.zeros_like(fold)
    fold[:, 0:NTHETA] = leg_ref[...].astype(F32)
    own = jnp.concatenate([fold[:, 0:512], fold[:, 512:1024]], axis=0).astype(BF16)
    mine_r, mine_c = row_slot(c, p, y), col_slot(z, h, c)
    slots[mine_r] = own
    slots[mine_c] = own

    started = []

    def copy_of(slot, peer, sem_at):
        return pltpu.make_async_remote_copy(
            src_ref=slots.at[slot], dst_ref=slots.at[slot],
            send_sem=send_sem.at[sem_at], recv_sem=slot_sem.at[slot],
            device_id=peer, device_id_type=MESH,
        )

    def send(slot, peer):
        copy = copy_of(slot, peer, len(started))
        copy.start()
        started.append(copy)

    def arrived(slot):
        copy_of(slot, sib, 0).wait_recv()

    pl.semaphore_wait(barrier, len(peers))

    send(mine_r, y_up)
    send(mine_r, y_down)
    send(mine_c, z_up)
    send(mine_c, z_down)
    send(mine_r, over_p)
    send(mine_c, over_h)
    send(mine_r, sib)
    send(mine_c, sib)

    codes[...] = jnp.zeros_like(codes)
    codes[0, 0:6, :] = code_ref[pl.ds((row // 2) * 6, 6), :].astype(F32)
    lane_at = lax.broadcasted_iota(jnp.int32, (128, 128), 1)
    source_at = lax.broadcasted_iota(jnp.int32, (128, 128), 0)
    all_codes = code_ref[...].astype(F32)
    for k in range(6):
        n = lane_at + k * 128
        i = (n * 2731) >> 16
        place = (i * 16 + col) * SUB + (n - i * SUB)
        pick = (source_at == (place & 127)).astype(F32)
        lanes = dot(all_codes, pick, 1, 0, lax.Precision.HIGHEST)
        keep = source_at[0:96] == (place >> 7)[0:96]
        codes[1, k : k + 1, :] = jnp.sum(jnp.where(keep, lanes, 0.0), axis=0, keepdims=True)
    code = jnp.round(codes[...])
    order = jnp.floor(code * 0.5)
    quarter = (code - 2.0 * order) * 0.25

    @pl.loop(0, 64)
    def _(b):
        angle = turns(order * b.astype(F32))
        cos_b[:, b] = cos_turns(angle)
        sin_b[:, b] = cos_turns(angle - 0.25)

    def trig_part(first, last):
        @pl.loop(first, last)
        def _(a):
            angle = turns(order * (a * 64).astype(F32)) - quarter
            cos_a, sin_a = cos_turns(angle), cos_turns(angle - 0.25)

            @pl.loop(0, 4)
            def _(b4):
                for u in range(16):
                    b = b4 * 16 + u
                    for q in range(2):
                        trig[q, a * 64 + b] = cos_a[q] * cos_b[q, b] - sin_a[q] * sin_b[q, b]

    def wide_part():
        @pl.loop(0, HALF // 128)
        def _(q):
            at = pl.ds(c * (HALF // 128) + q, 1)
            scale = weight_ref[at, :] * mask_ref[at, :].astype(F32)
            rows = pl.ds(pl.multiple_of(q * 128, 128), 128)
            s_wide[rows, :] = jnp.broadcast_to(scale, (128, 128)).T
            g_wide[rows, :] = jnp.broadcast_to(grad_ref[at, :], (128, 128)).T

    trig_part(0, 5)
    slot = row_slot(c, 1 - p, y)
    arrived(slot)
    send(slot, y_up)
    send(slot, y_down)
    send(slot, sib)
    slot = col_slot(z, 1 - h, c)
    arrived(slot)
    send(slot, z_up)
    send(slot, z_down)
    send(slot, sib)

    parts = iter([(5, 10), (10, 17), (17, 24), (24, 31), (31, 38), (38, 46), (46, 57)])
    for step in range(1, 4):
        for half in range(2):
            trig_part(*next(parts))
            if step == 3:
                pr, pc = half, half
            else:
                pr = p if half == 0 else 1 - p
                pc = h if half == 0 else 1 - h
            for up in (True, False):
                forward = step < 3 or (half == 0) == up
                off = 8 - step if up else step
                slot = row_slot(c, pr, (y + off) % 8)
                arrived(slot)
                if forward:
                    send(slot, y_up if up else y_down)
                send(slot, sib)
                slot = col_slot((z + off) % 8, pc, c)
                arrived(slot)
                if forward:
                    send(slot, z_up if up else z_down)
                send(slot, sib)
    trig_part(*next(parts))
    wide_part()
    for half in range(2):
        slot = row_slot(c, half, (y + 4) % 8)
        arrived(slot)
        send(slot, sib)
        slot = col_slot((z + 4) % 8, half, c)
        arrived(slot)
        send(slot, sib)

    @pl.loop(0, 16)
    def _(j):
        arrived((1 - c) * 16 + j)
        arrived(32 + j * 2 + (1 - c))

    eye = (
        lax.broadcasted_iota(jnp.int32, (256, 256), 0)
        == lax.broadcasted_iota(jnp.int32, (256, 256), 1)
    ).astype(BF16)
    flat = table.reshape(2 * 1024 * 8, 128)

    @pl.loop(0, 4)
    def _(group):
        block = slots[pl.ds(group * 16, 16)].astype(F32)
        base = (group // 2) * (1024 * 8) + (group % 2) * 3
        for half in range(2):
            x = block[:, half * SUB : (half + 1) * SUB, :].reshape(TILE, 512).astype(BF16)
            for q in range(2):
                turned = dot(eye, x[:, q * 256 : (q + 1) * 256], 1, 1)
                for k in range(3):
                    first = base + (half * 512 + q * 256) * 8 + k
                    flat[pl.ds(first, 256, stride=8), :] = turned[:, k * 128 : (k + 1) * 128]

    rhs_acc[...] = jnp.zeros_like(rhs_acc)

    def gather(blk):
        first = c * HALF + blk * BLOCK

        @pl.loop(0, BLOCK // 32)
        def _(b):
            at = pl.multiple_of(b * (32 * 12), 8)
            for u in range(32):
                t, l = colat_ref[first + b * 32 + u], lon_ref[first + b * 32 + u]
                gathered[pl.ds(at + u * 12, 8), :] = table[0, t] * trig[0, l]
                gathered[pl.ds(at + u * 12 + 6, 6), :] = (table[1, t] * trig[1, l])[0:6]

    def left_of(blk, half):
        rows = pl.ds(pl.multiple_of(blk * BLOCK, BLOCK), BLOCK)
        s, g = s_wide[rows, :], g_wide[rows, :]
        first = ((1 - c) if half == 0 else c) * 3
        parts = []
        for k in range(3):
            scaled = gathered[pl.ds(first + k, BLOCK, stride=12), :] * s
            rhs_acc[half, k] += jnp.sum((scaled * g).reshape(BLOCK // 8, 8, 128), axis=0)
            parts.append(scaled.astype(BF16))
        return jnp.concatenate(parts, axis=1)

    def right_of():
        return jnp.concatenate(
            [gathered[pl.ds(6 + k, BLOCK, stride=12), :].astype(BF16) for k in range(6)], axis=1
        )

    total[...] = jnp.zeros_like(total)

    @pl.loop(0, N_BLOCK - 1)
    def _(blk):
        gather(blk)
        left = jnp.concatenate([left_of(blk, 0), left_of(blk, 1)], axis=1)
        total[...] += dot(left, right_of(), 0, 0)

    last = N_BLOCK - 1
    gather(last)
    right = right_of()
    part[...] = (total[0:TILE, :] + dot(left_of(last, 0), right, 0, 0)).astype(BF16)
    far = pltpu.make_async_remote_copy(
        src_ref=part, dst_ref=far_ref, send_sem=send_sem.at[N_SEND], recv_sem=far_sem.at[0],
        device_id=sib, device_id_type=MESH,
    )
    far.start()
    own_ref[...] = total[TILE : 2 * TILE, :] + dot(left_of(last, 1), right, 0, 0)
    for k in range(3):
        lanes = slice(k * 128, (k + 1) * 128)
        rhs_part[:, lanes] = jnp.broadcast_to(
            jnp.sum(rhs_acc[0, k], axis=0, keepdims=True), (8, 128)
        )
        rhs_ref[:, lanes] = jnp.broadcast_to(
            jnp.sum(rhs_acc[1, k], axis=0, keepdims=True), (8, 128)
        )
    far_rhs = pltpu.make_async_remote_copy(
        src_ref=rhs_part, dst_ref=far_rhs_ref, send_sem=send_sem.at[N_SEND + 1],
        recv_sem=far_sem.at[1], device_id=sib, device_id_type=MESH,
    )
    far_rhs.start()
    for copy in started:
        copy.wait_send()
    far.wait()
    far_rhs.wait()


def shards(leg_table, coef_code, colat_idx, lon_idx, gap_mask, obs_weight, gradient):
    vmem, smem = pl.BlockSpec(memory_space=pltpu.VMEM), pl.BlockSpec(memory_space=pltpu.SMEM)
    hbm = pl.BlockSpec(memory_space=pl.ANY)
    own, own_rhs, far, far_rhs = pl.pallas_call(
        kernel,
        out_shape=(
            jax.ShapeDtypeStruct((TILE, 768), F32),
            jax.ShapeDtypeStruct((8, TILE), F32),
            jax.ShapeDtypeStruct((TILE, 768), BF16),
            jax.ShapeDtypeStruct((8, TILE), F32),
        ),
        in_specs=[vmem] * 5 + [smem] * 2,
        out_specs=(vmem, vmem, hbm, hbm),
        scratch_shapes=[
            pltpu.VMEM((64, 2 * SUB, 512), BF16),
            pltpu.VMEM((SUB, 1024), F32),
            pltpu.VMEM((2, 1024, 8, 128), F32),
            pltpu.VMEM((2, 57 * 64, 8, 128), F32),
            pltpu.VMEM((2, 64, 8, 128), F32),
            pltpu.VMEM((2, 64, 8, 128), F32),
            pltpu.VMEM((2, 8, 128), F32),
            pltpu.VMEM((BLOCK * 12, 128), F32),
            pltpu.VMEM((HALF, 128), F32),
            pltpu.VMEM((HALF, 128), F32),
            pltpu.VMEM((768, 768), F32),
            pltpu.VMEM((TILE, 768), BF16),
            pltpu.VMEM((2, 3, 8, 128), F32),
            pltpu.VMEM((8, TILE), F32),
            pltpu.SemaphoreType.DMA((N_SEND + 2,)),
            pltpu.SemaphoreType.DMA((64,)),
            pltpu.SemaphoreType.DMA((2,)),
        ],
        compiler_params=pltpu.CompilerParams(
            collective_id=0, has_side_effects=True, vmem_limit_bytes=62 * 2**20
        ),
    )(
        leg_table.T, coef_code.reshape(96, 128), gap_mask.reshape(48, 128),
        obs_weight.reshape(48, 128), gradient.reshape(48, 128), colat_idx, lon_idx,
    )
    normal = (own + far.astype(F32)) * (1.0 / OBS)
    rhs = (own_rhs[0] + far_rhs[0]) * (1.0 / OBS)
    return normal[None], rhs


def solution(mesh):
    placed = (P(None, ("row", "col")), P(), P(), P(), P(), P(), P())
    return jax.shard_map(
        shards,
        mesh=mesh,
        in_specs=placed,
        out_specs=(P("col", "row", None), P("row")),
        check_vma=False,
    )
```

```python
import functools

import jax
import jax.numpy as jnp
from jax import lax
from jax.experimental import pallas as pl
from jax.experimental.pallas import tpu as pltpu
from jax.sharding import PartitionSpec as P

NLON = 3600
NTHETA = 900
OBS = 6144
SUB = 24
HALF = OBS // 2
BLOCK = 1024
N_BLOCK = HALF // BLOCK
TILE = 384
F32 = jnp.float32
BF16 = jnp.bfloat16
MESH = pl.DeviceIdType.MESH
N_SEND = 62


def sin_turns(w):
    s = w * w
    p = -76.58128455924857 + s * 39.76072207493176
    p = 81.60248074286099 + s * p
    p = -41.341680668063056 + s * p
    p = 6.283185280261415 + s * p
    return w * p


def cos_turns(f):
    return sin_turns(0.25 - jnp.abs(f - jnp.round(f)))


def turns(x):
    return (x - NLON * jnp.round(x * (1.0 / NLON))) * (1.0 / NLON)


def dot(a, b, ca, cb, precision=None):
    return lax.dot_general(
        a, b, (((ca,), (cb,)), ((), ())), preferred_element_type=F32, precision=precision
    )


def kernel(
    leg_hbm, code_hbm, mask_hbm, weight_hbm, grad_hbm, colat_hbm, lon_hbm,
    own_ref, rhs_ref, far_ref, far_rhs_ref,
    slots, leg_ref, fold, table, wave, trig_a, trig_b, codes, gathered,
    total, part, rhs_acc, rhs_part, code_ref, mask_ref, weight_ref, scale_ref, grad_ref, colat_ref, lon_ref,
    send_sem, slot_sem, far_sem, load_sem,
):
    row, col = lax.axis_index("row"), lax.axis_index("col")
    z, h, c = row // 4, (row // 2) % 2, row % 2
    p, y = col // 8, col % 8

    def rid(z_, h_, c_):
        return z_ * 4 + h_ * 2 + c_

    def cid(p_, y_):
        return p_ * 8 + y_

    sib = (rid(z, h, 1 - c), col)
    over_p = (row, cid(1 - p, y))
    over_h = (rid(z, 1 - h, c), col)

    def along_y(off):
        return (row, cid(p, (y + off % 8) % 8))

    def along_z(off):
        return (rid((z + off % 8) % 8, h, c), col)

    near = (1, 2, -1, -2)
    peers = (sib, over_p, over_h) + tuple(along_y(o) for o in near) + tuple(along_z(o) for o in near)

    barrier = pltpu.get_barrier_semaphore()
    for peer in peers:
        pl.semaphore_signal(barrier, inc=1, device_id=peer, device_id_type=MESH)

    my_half = pl.ds(pl.multiple_of(c * HALF, HALF), HALF)
    my_rows = pl.ds(pl.multiple_of(c * (HALF // 128), 8), HALF // 128)
    loads = [
        pltpu.make_async_copy(src, dst, load_sem.at[n])
        for n, (src, dst) in enumerate((
            (leg_hbm, leg_ref), (code_hbm, code_ref), (lon_hbm.at[my_half], lon_ref),
            (colat_hbm.at[my_half], colat_ref), (weight_hbm.at[my_rows], weight_ref),
            (mask_hbm.at[my_rows], mask_ref), (grad_hbm.at[my_half], grad_ref),
        ))
    ]
    for load in loads:
        load.start()

    def row_slot(core, plane, y_):
        return core * 16 + plane * 8 + y_

    def col_slot(z_, plane, core):
        return 32 + z_ * 4 + plane * 2 + core

    fold[...] = jnp.zeros_like(fold)
    loads[0].wait()
    fold[:, 0:NTHETA] = leg_ref[...].astype(F32)
    own = jnp.concatenate([fold[:, 0:512], fold[:, 512:1024]], axis=0).astype(BF16)
    mine_r, mine_c = row_slot(c, p, y), col_slot(z, h, c)
    slots[mine_r] = own
    slots[mine_c] = own

    started = []

    def copy_of(slot, peer, sem_at):
        return pltpu.make_async_remote_copy(
            src_ref=slots.at[slot], dst_ref=slots.at[slot],
            send_sem=send_sem.at[sem_at], recv_sem=slot_sem.at[slot],
            device_id=peer, device_id_type=MESH,
        )

    def send(slot, peer):
        copy = copy_of(slot, peer, len(started))
        copy.start()
        started.append(copy)

    def arrived(slot):
        copy_of(slot, sib, 0).wait_recv()

    pl.semaphore_wait(barrier, len(peers))

    for off in (2, -2):
        send(mine_r, along_y(off))
        send(mine_c, along_z(off))
    send(mine_r, over_p)
    send(mine_c, over_h)
    for off in (1, -1):
        send(mine_r, along_y(off))
        send(mine_c, along_z(off))
    send(mine_r, sib)
    send(mine_c, sib)
    for load in loads[1:]:
        load.wait()
    weight_ref[...] = weight_ref[...] * mask_ref[...].astype(F32)
    to_scalars = pltpu.make_async_copy(weight_ref, scale_ref, load_sem.at[7])
    to_scalars.start()

    codes[...] = jnp.zeros_like(codes)
    codes[0, 0:6, :] = code_ref[pl.ds((row // 2) * 6, 6), :].astype(F32)
    lane_at = lax.broadcasted_iota(jnp.int32, (128, 128), 1)
    source_at = lax.broadcasted_iota(jnp.int32, (128, 128), 0)
    all_codes = code_ref[...].astype(F32)
    for k in range(6):
        n = lane_at + k * 128
        i = (n * 2731) >> 16
        place = (i * 16 + col) * SUB + (n - i * SUB)
        pick = (source_at == (place & 127)).astype(F32)
        lanes = dot(all_codes, pick, 1, 0, lax.Precision.HIGHEST)
        keep = source_at[0:96] == (place >> 7)[0:96]
        codes[1, k : k + 1, :] = jnp.sum(jnp.where(keep, lanes, 0.0), axis=0, keepdims=True)
    code = jnp.round(codes[...])
    order = jnp.floor(code * 0.5)
    quarter = (code - 2.0 * order) * 0.25

    @pl.loop(0, 64)
    def _(n):
        angle = turns(order * n.astype(F32))
        trig_b[n, 0:2] = cos_turns(angle)
        trig_b[n, 2:4] = cos_turns(angle - 0.25)
        angle = turns(order * (n * 64).astype(F32)) - quarter
        trig_a[n, 0:2] = cos_turns(angle)
        trig_a[n, 2:4] = cos_turns(angle - 0.25)

    to_scalars.wait()

    def wave_part(first, last):
        @pl.loop(first // 32, last // 32)
        def _(n):
            lane = (n % 4) * 32
            for u in range(32):
                at = n * 32 + u
                l = lon_ref[at]
                a, b = l >> 6, l & 63
                rows = trig_a[a, 0] * trig_b[b, 0] - trig_a[a, 2] * trig_b[b, 2]
                wave[at, 0] = rows * scale_ref[n // 4, lane + u]
                wave[at, 1] = trig_a[a, 1] * trig_b[b, 1] - trig_a[a, 3] * trig_b[b, 3]

    def row_at(own_plane, off):
        return row_slot(c, p if own_plane else 1 - p, (y + off % 8) % 8)

    def col_at(own_plane, off):
        return col_slot((z + off % 8) % 8, h if own_plane else 1 - h, c)

    ways = ((row_at, along_y), (col_at, along_z))

    def take(slot, *onward):
        arrived(slot)
        for peer in onward:
            send(slot, peer)
        send(slot, sib)

    def second_stage(own_plane):
        for at, along in ways:
            onward = (along(2), along(1)) if own_plane else (along(1),)
            take(at(own_plane, -2), *onward)
        for at, along in ways:
            onward = (along(-1),) if own_plane else (along(-2), along(-1))
            take(at(own_plane, 2), *onward)

    def take_all(own_plane, offs):
        for off in offs:
            for at, _ in ways:
                take(at(own_plane, off))

    for at, along in ways:
        take(at(False, 0), along(2), along(-2), along(1), along(-1))
    wave_part(0, 416)
    second_stage(True)
    wave_part(416, 1376)
    second_stage(False)
    wave_part(1376, 2016)
    take_all(True, (1, -1))
    take_all(False, (1, -1))
    take_all(True, (3, -3, 4))
    wave_part(2016, 3072)
    take_all(False, (3, -3, 4))
    for copy in started[:40]:
        copy.wait_send()

    eye = (
        lax.broadcasted_iota(jnp.int32, (256, 256), 0)
        == lax.broadcasted_iota(jnp.int32, (256, 256), 1)
    ).astype(BF16)
    flat = table.reshape(2 * 1024 * 8, 128)

    def build(group):
        block = slots[pl.ds(group * 16, 16)].astype(F32)
        base = (group // 2) * (1024 * 8) + (group % 2) * 3
        for half in range(2):
            x = block[:, half * SUB : (half + 1) * SUB, :].reshape(TILE, 512).astype(BF16)
            for q in range(2):
                turned = dot(eye, x[:, q * 256 : (q + 1) * 256], 1, 1)
                for k in range(3):
                    first = base + (half * 512 + q * 256) * 8 + k
                    flat[pl.ds(first, 256, stride=8), :] = turned[:, k * 128 : (k + 1) * 128]

    build(c)

    @pl.loop(0, 16)
    def _(j):
        arrived((1 - c) * 16 + j)
        arrived(32 + j * 2 + (1 - c))

    @pl.loop(0, 3)
    def _(n):
        build(jnp.where(n == 0, 1 - c, n + 1))

    rhs_acc[...] = jnp.zeros_like(rhs_acc)

    def gather(blk):
        first = blk * BLOCK

        def some(b, acc):
            at = pl.multiple_of(b * (32 * 12), 8)
            for u in range(32):
                o = first + b * 32 + u
                t = colat_ref[o]
                scaled = table[0, t] * wave[o, 0]
                gathered[pl.ds(at + u * 12, 8), :] = scaled
                gathered[pl.ds(at + u * 12 + 6, 6), :] = (table[1, t] * wave[o, 1])[0:6]
                acc = acc + scaled * grad_ref[o]
            return acc

        rhs_acc[...] = lax.fori_loop(0, BLOCK // 32, some, rhs_acc[...])

    def left_of(half):
        first = ((1 - c) if half == 0 else c) * 3
        return jnp.concatenate(
            [gathered[pl.ds(first + k, BLOCK, stride=12), :].astype(BF16) for k in range(3)], axis=1
        )

    def right_of():
        return jnp.concatenate(
            [gathered[pl.ds(6 + k, BLOCK, stride=12), :].astype(BF16) for k in range(6)], axis=1
        )

    total[...] = jnp.zeros_like(total)

    @pl.loop(0, N_BLOCK - 1)
    def _(blk):
        gather(blk)
        left = jnp.concatenate([left_of(0), left_of(1)], axis=1)
        total[...] += dot(left, right_of(), 0, 0)

    last = N_BLOCK - 1
    gather(last)
    right = right_of()
    part[...] = (total[0:TILE, :] + dot(left_of(0), right, 0, 0)).astype(BF16)
    far = pltpu.make_async_remote_copy(
        src_ref=part, dst_ref=far_ref, send_sem=send_sem.at[N_SEND], recv_sem=far_sem.at[0],
        device_id=sib, device_id_type=MESH,
    )
    far.start()
    total[TILE : 2 * TILE, :] += dot(left_of(1), right, 0, 0)
    near_copy = pltpu.make_async_copy(total.at[pl.ds(TILE, TILE)], own_ref, load_sem.at[0])
    near_copy.start()
    rhs_part[...] = jnp.zeros_like(rhs_part)
    rhs_ref[...] = jnp.zeros_like(rhs_ref)
    rhs_part[0:3, :] = rhs_acc[pl.ds((1 - c) * 3, 3), :]
    rhs_ref[0:3, :] = rhs_acc[pl.ds(c * 3, 3), :]
    far_rhs = pltpu.make_async_remote_copy(
        src_ref=rhs_part, dst_ref=far_rhs_ref, send_sem=send_sem.at[N_SEND + 1],
        recv_sem=far_sem.at[1], device_id=sib, device_id_type=MESH,
    )
    far_rhs.start()
    for copy in started[40:]:
        copy.wait_send()
    near_copy.wait()
    far_rhs.wait()
    far.wait()


def finish(own_ref, rhs_ref, far_ref, far_rhs_ref, normal_ref, sum_ref):
    normal_ref[0] = (own_ref[...] + far_ref[...].astype(F32)) * (1.0 / OBS)

    @pl.when(pl.program_id(0) == 0)
    def _():
        sum_ref[...] = ((rhs_ref[0:3, :] + far_rhs_ref[0:3, :]) * (1.0 / OBS)).reshape(TILE)


def shards(leg_table, coef_code, colat_idx, lon_idx, gap_mask, obs_weight, gradient):
    vmem = pl.BlockSpec(memory_space=pltpu.VMEM)
    hbm = pl.BlockSpec(memory_space=pl.ANY)
    own, own_rhs, far, far_rhs = pl.pallas_call(
        kernel,
        out_shape=(
            jax.ShapeDtypeStruct((TILE, 768), F32),
            jax.ShapeDtypeStruct((8, 128), F32),
            jax.ShapeDtypeStruct((TILE, 768), BF16),
            jax.ShapeDtypeStruct((8, 128), F32),
        ),
        in_specs=[hbm] * 7,
        out_specs=(hbm, vmem, hbm, hbm),
        scratch_shapes=[
            pltpu.VMEM((64, 2 * SUB, 512), BF16),
            pltpu.VMEM((SUB, NTHETA), BF16),
            pltpu.VMEM((SUB, 1024), F32),
            pltpu.VMEM((2, 1024, 8, 128), F32),
            pltpu.VMEM((HALF, 2, 8, 128), F32),
            pltpu.VMEM((64, 4, 8, 128), F32),
            pltpu.VMEM((64, 4, 8, 128), F32),
            pltpu.VMEM((2, 8, 128), F32),
            pltpu.VMEM((BLOCK * 12, 128), F32),
            pltpu.VMEM((768, 768), F32),
            pltpu.VMEM((TILE, 768), BF16),
            pltpu.VMEM((8, 128), F32),
            pltpu.VMEM((8, 128), F32),
            pltpu.VMEM((96, 128), jnp.int32),
            pltpu.VMEM((HALF // 128, 128), jnp.int32),
            pltpu.VMEM((HALF // 128, 128), F32),
            pltpu.SMEM((HALF // 128, 128), F32),
            pltpu.SMEM((HALF,), F32),
            pltpu.SMEM((HALF,), jnp.int32),
            pltpu.SMEM((HALF,), jnp.int32),
            pltpu.SemaphoreType.DMA((N_SEND + 2,)),
            pltpu.SemaphoreType.DMA((64,)),
            pltpu.SemaphoreType.DMA((2,)),
            pltpu.SemaphoreType.DMA((8,)),
        ],
        compiler_params=pltpu.CompilerParams(
            collective_id=0, has_side_effects=True, vmem_limit_bytes=62 * 2**20
        ),
    )(
        leg_table.T, coef_code.reshape(96, 128), gap_mask.reshape(48, 128),
        obs_weight.reshape(48, 128), gradient, colat_idx, lon_idx,
    )
    half = TILE // 2
    normal, rhs = pl.pallas_call(
        finish,
        grid=(2,),
        in_specs=[
            pl.BlockSpec((half, 768), lambda i: (i, 0)),
            pl.BlockSpec((8, 128), lambda i: (0, 0)),
            pl.BlockSpec((half, 768), lambda i: (i, 0)),
            pl.BlockSpec((8, 128), lambda i: (0, 0)),
        ],
        out_specs=(
            pl.BlockSpec((1, half, 768), lambda i: (0, i, 0)),
            pl.BlockSpec((TILE,), lambda i: (0,)),
        ),
        out_shape=(
            jax.ShapeDtypeStruct((1, TILE, 768), F32),
            jax.ShapeDtypeStruct((TILE,), F32),
        ),
    )(own, own_rhs, far, far_rhs)
    return normal, rhs


def solution(mesh):
    placed = (P(None, ("row", "col")), P(), P(), P(), P(), P(), P())
    return jax.shard_map(
        shards,
        mesh=mesh,
        in_specs=placed,
        out_specs=(P("col", "row", None), P("row")),
        check_vma=False,
    )
```

```python
import functools

import jax
import jax.numpy as jnp
from jax import lax
from jax.experimental import pallas as pl
from jax.experimental.pallas import tpu as pltpu
from jax.sharding import PartitionSpec as P

NLON = 3600
NTHETA = 900
OBS = 6144
SUB = 24
HALF = OBS // 2
BLOCK = 1024
N_BLOCK = HALF // BLOCK
TILE = 384
F32 = jnp.float32
BF16 = jnp.bfloat16
MESH = pl.DeviceIdType.MESH
N_SEND = 62


def sin_turns(w):
    s = w * w
    p = -76.58128455924857 + s * 39.76072207493176
    p = 81.60248074286099 + s * p
    p = -41.341680668063056 + s * p
    p = 6.283185280261415 + s * p
    return w * p


def cos_turns(f):
    return sin_turns(0.25 - jnp.abs(f - jnp.round(f)))


def turns(x):
    return (x - NLON * jnp.round(x * (1.0 / NLON))) * (1.0 / NLON)


def dot(a, b, ca, cb, precision=None):
    return lax.dot_general(
        a, b, (((ca,), (cb,)), ((), ())), preferred_element_type=F32, precision=precision
    )


def kernel(
    leg_hbm, code_hbm, mask_hbm, weight_hbm, grad_hbm, colat_hbm, lon_hbm,
    own_ref, rhs_ref, far_ref, far_rhs_ref,
    slots, leg_ref, fold, table, wave, trig_a, trig_b, codes, gathered,
    total, part, rhs_acc, rhs_part, code_ref, mask_ref, weight_ref, scale_ref, grad_ref, colat_ref, lon_ref,
    send_sem, slot_sem, far_sem, load_sem,
):
    row, col = lax.axis_index("row"), lax.axis_index("col")
    z, h, c = row // 4, (row // 2) % 2, row % 2
    p, y = col // 8, col % 8

    def rid(z_, h_, c_):
        return z_ * 4 + h_ * 2 + c_

    def cid(p_, y_):
        return p_ * 8 + y_

    sib = (rid(z, h, 1 - c), col)
    over_p = (row, cid(1 - p, y))
    over_h = (rid(z, 1 - h, c), col)

    def along_y(off):
        return (row, cid(p, (y + off % 8) % 8))

    def along_z(off):
        return (rid((z + off % 8) % 8, h, c), col)

    near = (1, 2, -1, -2)
    peers = (sib, over_p, over_h) + tuple(along_y(o) for o in near) + tuple(along_z(o) for o in near)

    barrier = pltpu.get_barrier_semaphore()
    for peer in peers:
        pl.semaphore_signal(barrier, inc=1, device_id=peer, device_id_type=MESH)

    my_half = pl.ds(pl.multiple_of(c * HALF, HALF), HALF)
    my_rows = pl.ds(pl.multiple_of(c * (HALF // 128), 8), HALF // 128)
    loads = [
        pltpu.make_async_copy(src, dst, load_sem.at[n])
        for n, (src, dst) in enumerate((
            (leg_hbm, leg_ref), (code_hbm, code_ref), (lon_hbm.at[my_half], lon_ref),
            (colat_hbm.at[my_half], colat_ref), (weight_hbm.at[my_rows], weight_ref),
            (mask_hbm.at[my_rows], mask_ref), (grad_hbm.at[my_half], grad_ref),
        ))
    ]
    for load in loads:
        load.start()

    def row_slot(core, plane, y_):
        return core * 16 + plane * 8 + y_

    def col_slot(z_, plane, core):
        return 32 + z_ * 4 + plane * 2 + core

    fold[...] = jnp.zeros_like(fold)
    loads[0].wait()
    fold[:, 0:NTHETA] = leg_ref[...].astype(F32)
    own = jnp.concatenate([fold[:, 0:512], fold[:, 512:1024]], axis=0).astype(BF16)
    mine_r, mine_c = row_slot(c, p, y), col_slot(z, h, c)
    slots[mine_r] = own
    slots[mine_c] = own

    started = []

    def copy_of(slot, peer, sem_at):
        return pltpu.make_async_remote_copy(
            src_ref=slots.at[slot], dst_ref=slots.at[slot],
            send_sem=send_sem.at[sem_at], recv_sem=slot_sem.at[slot],
            device_id=peer, device_id_type=MESH,
        )

    def send(slot, peer):
        copy = copy_of(slot, peer, len(started))
        copy.start()
        started.append(copy)

    def arrived(slot):
        copy_of(slot, sib, 0).wait_recv()

    pl.semaphore_wait(barrier, len(peers))

    for off in (2, -2):
        send(mine_r, along_y(off))
        send(mine_c, along_z(off))
    send(mine_r, over_p)
    send(mine_c, over_h)
    for off in (1, -1):
        send(mine_r, along_y(off))
        send(mine_c, along_z(off))
    send(mine_r, sib)
    send(mine_c, sib)
    for load in loads[1:]:
        load.wait()
    weight_ref[...] = weight_ref[...] * mask_ref[...].astype(F32)
    to_scalars = pltpu.make_async_copy(weight_ref, scale_ref, load_sem.at[7])
    to_scalars.start()

    codes[...] = jnp.zeros_like(codes)
    codes[0, 0:6, :] = code_ref[pl.ds((row // 2) * 6, 6), :].astype(F32)
    lane_at = lax.broadcasted_iota(jnp.int32, (128, 128), 1)
    source_at = lax.broadcasted_iota(jnp.int32, (128, 128), 0)
    all_codes = code_ref[...].astype(F32)
    for k in range(6):
        n = lane_at + k * 128
        i = (n * 2731) >> 16
        place = (i * 16 + col) * SUB + (n - i * SUB)
        pick = (source_at == (place & 127)).astype(F32)
        lanes = dot(all_codes, pick, 1, 0, lax.Precision.HIGHEST)
        keep = source_at[0:96] == (place >> 7)[0:96]
        codes[1, k : k + 1, :] = jnp.sum(jnp.where(keep, lanes, 0.0), axis=0, keepdims=True)
    code = jnp.round(codes[...])
    order = jnp.floor(code * 0.5)
    quarter = (code - 2.0 * order) * 0.25

    @pl.loop(0, 16)
    def _(n4):
        for u in range(4):
            n = n4 * 4 + u
            angle = turns(order * n.astype(F32))
            trig_b[n, 0:2] = cos_turns(angle)
            trig_b[n, 2:4] = cos_turns(angle - 0.25)
            angle = turns(order * (n * 64).astype(F32)) - quarter
            trig_a[n, 0:2] = cos_turns(angle)
            trig_a[n, 2:4] = cos_turns(angle - 0.25)

    to_scalars.wait()

    def wave_part(first, last):
        @pl.loop(first // 128, last // 128)
        def _(n):
            for u in range(128):
                at = n * 128 + u
                l = lon_ref[at]
                a, b = l >> 6, l & 63
                rows = trig_a[a, 0] * trig_b[b, 0] - trig_a[a, 2] * trig_b[b, 2]
                wave[at, 0] = rows * scale_ref[n, u]
                wave[at, 1] = trig_a[a, 1] * trig_b[b, 1] - trig_a[a, 3] * trig_b[b, 3]

    def row_at(own_plane, off):
        return row_slot(c, p if own_plane else 1 - p, (y + off % 8) % 8)

    def col_at(own_plane, off):
        return col_slot((z + off % 8) % 8, h if own_plane else 1 - h, c)

    ways = ((row_at, along_y), (col_at, along_z))

    def take(slot, *onward):
        arrived(slot)
        for peer in onward:
            send(slot, peer)
        send(slot, sib)

    def second_stage(own_plane):
        for at, along in ways:
            onward = (along(2), along(1)) if own_plane else (along(1),)
            take(at(own_plane, -2), *onward)
        for at, along in ways:
            onward = (along(-1),) if own_plane else (along(-2), along(-1))
            take(at(own_plane, 2), *onward)

    def take_all(own_plane, offs):
        for off in offs:
            for at, _ in ways:
                take(at(own_plane, off))

    for at, along in ways:
        take(at(False, 0), along(2), along(-2), along(1), along(-1))
    wave_part(0, 384)
    second_stage(True)
    wave_part(384, 1408)
    second_stage(False)
    wave_part(1408, 2048)
    take_all(True, (1, -1))
    take_all(False, (1, -1))
    take_all(True, (3, -3, 4))
    wave_part(2048, 3072)
    take_all(False, (3, -3, 4))
    for copy in started[:40]:
        copy.wait_send()

    eye = (
        lax.broadcasted_iota(jnp.int32, (256, 256), 0)
        == lax.broadcasted_iota(jnp.int32, (256, 256), 1)
    ).astype(BF16)
    flat = table.reshape(2 * 1024 * 8, 128)

    def build(group):
        block = slots[pl.ds(group * 16, 16)].astype(F32)
        base = (group // 2) * (1024 * 8) + (group % 2) * 3
        for half in range(2):
            x = block[:, half * SUB : (half + 1) * SUB, :].reshape(TILE, 512).astype(BF16)
            for q in range(2):
                turned = dot(eye, x[:, q * 256 : (q + 1) * 256], 1, 1)
                for k in range(3):
                    first = base + (half * 512 + q * 256) * 8 + k
                    flat[pl.ds(first, 256, stride=8), :] = turned[:, k * 128 : (k + 1) * 128]

    build(c)

    @pl.loop(0, 16)
    def _(j):
        arrived((1 - c) * 16 + j)
        arrived(32 + j * 2 + (1 - c))

    @pl.loop(0, 3)
    def _(n):
        build(jnp.where(n == 0, 1 - c, n + 1))

    rhs_acc[...] = jnp.zeros_like(rhs_acc)

    def gather(blk):
        first = blk * BLOCK

        def some(b, acc):
            at = pl.multiple_of(b * (32 * 12), 8)
            for u in range(32):
                o = first + b * 32 + u
                t = colat_ref[o]
                scaled = table[0, t] * wave[o, 0]
                gathered[pl.ds(at + u * 12, 8), :] = scaled
                gathered[pl.ds(at + u * 12 + 6, 6), :] = (table[1, t] * wave[o, 1])[0:6]
                acc = acc + scaled * grad_ref[o]
            return acc

        rhs_acc[...] = lax.fori_loop(0, BLOCK // 32, some, rhs_acc[...])

    def left_of(half):
        first = ((1 - c) if half == 0 else c) * 3
        return jnp.concatenate(
            [gathered[pl.ds(first + k, BLOCK, stride=12), :].astype(BF16) for k in range(3)], axis=1
        )

    def right_of():
        return jnp.concatenate(
            [gathered[pl.ds(6 + k, BLOCK, stride=12), :].astype(BF16) for k in range(6)], axis=1
        )

    total[...] = jnp.zeros_like(total)

    @pl.loop(0, N_BLOCK - 1)
    def _(blk):
        gather(blk)
        left = jnp.concatenate([left_of(0), left_of(1)], axis=1)
        total[...] += dot(left, right_of(), 0, 0)

    last = N_BLOCK - 1
    gather(last)
    right = right_of()
    part[...] = (total[0:TILE, :] + dot(left_of(0), right, 0, 0)).astype(BF16)
    far = pltpu.make_async_remote_copy(
        src_ref=part, dst_ref=far_ref, send_sem=send_sem.at[N_SEND], recv_sem=far_sem.at[0],
        device_id=sib, device_id_type=MESH,
    )
    far.start()
    total[TILE : 2 * TILE, :] += dot(left_of(1), right, 0, 0)
    near_copy = pltpu.make_async_copy(total.at[pl.ds(TILE, TILE)], own_ref, load_sem.at[0])
    near_copy.start()
    rhs_part[...] = jnp.zeros_like(rhs_part)
    rhs_ref[...] = jnp.zeros_like(rhs_ref)
    rhs_part[0:3, :] = rhs_acc[pl.ds((1 - c) * 3, 3), :]
    rhs_ref[0:3, :] = rhs_acc[pl.ds(c * 3, 3), :]
    far_rhs = pltpu.make_async_remote_copy(
        src_ref=rhs_part, dst_ref=far_rhs_ref, send_sem=send_sem.at[N_SEND + 1],
        recv_sem=far_sem.at[1], device_id=sib, device_id_type=MESH,
    )
    far_rhs.start()
    for copy in started[40:]:
        copy.wait_send()
    near_copy.wait()
    far_rhs.wait()
    far.wait()


def finish(own_ref, rhs_ref, far_ref, far_rhs_ref, normal_ref, sum_ref):
    normal_ref[0] = (own_ref[...] + far_ref[...].astype(F32)) * (1.0 / OBS)

    @pl.when(pl.program_id(0) == 0)
    def _():
        sum_ref[...] = ((rhs_ref[0:3, :] + far_rhs_ref[0:3, :]) * (1.0 / OBS)).reshape(TILE)


def shards(leg_table, coef_code, colat_idx, lon_idx, gap_mask, obs_weight, gradient):
    vmem = pl.BlockSpec(memory_space=pltpu.VMEM)
    hbm = pl.BlockSpec(memory_space=pl.ANY)
    own, own_rhs, far, far_rhs = pl.pallas_call(
        kernel,
        out_shape=(
            jax.ShapeDtypeStruct((TILE, 768), F32),
            jax.ShapeDtypeStruct((8, 128), F32),
            jax.ShapeDtypeStruct((TILE, 768), BF16),
            jax.ShapeDtypeStruct((8, 128), F32),
        ),
        in_specs=[hbm] * 7,
        out_specs=(hbm, vmem, hbm, hbm),
        scratch_shapes=[
            pltpu.VMEM((64, 2 * SUB, 512), BF16),
            pltpu.VMEM((SUB, NTHETA), BF16),
            pltpu.VMEM((SUB, 1024), F32),
            pltpu.VMEM((2, 1024, 8, 128), F32),
            pltpu.VMEM((HALF, 2, 8, 128), F32),
            pltpu.VMEM((64, 4, 8, 128), F32),
            pltpu.VMEM((64, 4, 8, 128), F32),
            pltpu.VMEM((2, 8, 128), F32),
            pltpu.VMEM((BLOCK * 12, 128), F32),
            pltpu.VMEM((768, 768), F32),
            pltpu.VMEM((TILE, 768), BF16),
            pltpu.VMEM((8, 128), F32),
            pltpu.VMEM((8, 128), F32),
            pltpu.VMEM((96, 128), jnp.int32),
            pltpu.VMEM((HALF // 128, 128), jnp.int32),
            pltpu.VMEM((HALF // 128, 128), F32),
            pltpu.SMEM((HALF // 128, 128), F32),
            pltpu.SMEM((HALF,), F32),
            pltpu.SMEM((HALF,), jnp.int32),
            pltpu.SMEM((HALF,), jnp.int32),
            pltpu.SemaphoreType.DMA((N_SEND + 2,)),
            pltpu.SemaphoreType.DMA((64,)),
            pltpu.SemaphoreType.DMA((2,)),
            pltpu.SemaphoreType.DMA((8,)),
        ],
        compiler_params=pltpu.CompilerParams(
            collective_id=0, has_side_effects=True, vmem_limit_bytes=62 * 2**20
        ),
    )(
        leg_table.T, coef_code.reshape(96, 128), gap_mask.reshape(48, 128),
        obs_weight.reshape(48, 128), gradient, colat_idx, lon_idx,
    )
    half = TILE // 2
    normal, rhs = pl.pallas_call(
        finish,
        grid=(2,),
        in_specs=[
            pl.BlockSpec((half, 768), lambda i: (i, 0)),
            pl.BlockSpec((8, 128), lambda i: (0, 0)),
            pl.BlockSpec((half, 768), lambda i: (i, 0)),
            pl.BlockSpec((8, 128), lambda i: (0, 0)),
        ],
        out_specs=(
            pl.BlockSpec((1, half, 768), lambda i: (0, i, 0)),
            pl.BlockSpec((TILE,), lambda i: (0,)),
        ),
        out_shape=(
            jax.ShapeDtypeStruct((1, TILE, 768), F32),
            jax.ShapeDtypeStruct((TILE,), F32),
        ),
    )(own, own_rhs, far, far_rhs)
    return normal, rhs


def solution(mesh):
    placed = (P(None, ("row", "col")), P(), P(), P(), P(), P(), P())
    return jax.shard_map(
        shards,
        mesh=mesh,
        in_specs=placed,
        out_specs=(P("col", "row", None), P("row")),
        check_vma=False,
    )
```

```python
import functools

import jax
import jax.numpy as jnp
from jax import lax
from jax.experimental import pallas as pl
from jax.experimental.pallas import tpu as pltpu
from jax.sharding import PartitionSpec as P

NLON = 3600
NTHETA = 900
OBS = 6144
SUB = 24
HALF = OBS // 2
BLOCK = 1024
N_BLOCK = HALF // BLOCK
TILE = 384
F32 = jnp.float32
BF16 = jnp.bfloat16
MESH = pl.DeviceIdType.MESH
N_SEND = 62


def sin_turns(w):
    s = w * w
    p = -76.58128455924857 + s * 39.76072207493176
    p = 81.60248074286099 + s * p
    p = -41.341680668063056 + s * p
    p = 6.283185280261415 + s * p
    return w * p


def cos_turns(f):
    return sin_turns(0.25 - jnp.abs(f - jnp.round(f)))


def turns(x):
    return (x - NLON * jnp.round(x * (1.0 / NLON))) * (1.0 / NLON)


def dot(a, b, ca, cb, precision=None):
    return lax.dot_general(
        a, b, (((ca,), (cb,)), ((), ())), preferred_element_type=F32, precision=precision
    )


def kernel(
    leg_hbm, code_hbm, mask_hbm, weight_hbm, grad_hbm, colat_hbm, lon_hbm,
    own_ref, rhs_ref, far_ref, far_rhs_ref,
    slots, leg_ref, fold, table, wave, trig_a, trig_b, codes, gathered,
    total, part, rhs_acc, rhs_part, code_ref, mask_ref, weight_ref, scale_ref, grad_ref, colat_ref, lon_ref,
    send_sem, slot_sem, far_sem, load_sem,
):
    row, col = lax.axis_index("row"), lax.axis_index("col")
    z, h, c = row // 4, (row // 2) % 2, row % 2
    p, y = col // 8, col % 8

    def rid(z_, h_, c_):
        return z_ * 4 + h_ * 2 + c_

    def cid(p_, y_):
        return p_ * 8 + y_

    sib = (rid(z, h, 1 - c), col)
    over_p = (row, cid(1 - p, y))
    over_h = (rid(z, 1 - h, c), col)

    def along_y(off):
        return (row, cid(p, (y + off % 8) % 8))

    def along_z(off):
        return (rid((z + off % 8) % 8, h, c), col)

    near = (1, 2, -1, -2)
    peers = (sib, over_p, over_h) + tuple(along_y(o) for o in near) + tuple(along_z(o) for o in near)

    barrier = pltpu.get_barrier_semaphore()
    for peer in peers:
        pl.semaphore_signal(barrier, inc=1, device_id=peer, device_id_type=MESH)

    my_half = pl.ds(pl.multiple_of(c * HALF, HALF), HALF)
    my_rows = pl.ds(pl.multiple_of(c * (HALF // 128), 8), HALF // 128)
    loads = [
        pltpu.make_async_copy(src, dst, load_sem.at[n])
        for n, (src, dst) in enumerate((
            (leg_hbm, leg_ref), (code_hbm, code_ref), (lon_hbm.at[my_half], lon_ref),
            (colat_hbm.at[my_half], colat_ref), (weight_hbm.at[my_rows], weight_ref),
            (mask_hbm.at[my_rows], mask_ref), (grad_hbm.at[my_half], grad_ref),
        ))
    ]
    for load in loads:
        load.start()

    def row_slot(core, plane, y_):
        return core * 16 + plane * 8 + y_

    def col_slot(z_, plane, core):
        return 32 + z_ * 4 + plane * 2 + core

    fold[...] = jnp.zeros_like(fold)
    loads[0].wait()
    fold[:, 0:NTHETA] = leg_ref[...].astype(F32)
    own = jnp.concatenate([fold[:, 0:512], fold[:, 512:1024]], axis=0).astype(BF16)
    mine_r, mine_c = row_slot(c, p, y), col_slot(z, h, c)
    slots[mine_r] = own
    slots[mine_c] = own

    started = []

    def copy_of(slot, peer, sem_at):
        return pltpu.make_async_remote_copy(
            src_ref=slots.at[slot], dst_ref=slots.at[slot],
            send_sem=send_sem.at[sem_at], recv_sem=slot_sem.at[slot],
            device_id=peer, device_id_type=MESH,
        )

    def send(slot, peer):
        copy = copy_of(slot, peer, len(started))
        copy.start()
        started.append(copy)

    def arrived(slot):
        copy_of(slot, sib, 0).wait_recv()

    pl.semaphore_wait(barrier, len(peers))

    for off in (2, -2):
        send(mine_r, along_y(off))
        send(mine_c, along_z(off))
    send(mine_r, over_p)
    send(mine_c, over_h)
    for off in (1, -1):
        send(mine_r, along_y(off))
        send(mine_c, along_z(off))
    send(mine_r, sib)
    send(mine_c, sib)
    for load in loads[1:]:
        load.wait()
    weight_ref[...] = weight_ref[...] * mask_ref[...].astype(F32)
    to_scalars = pltpu.make_async_copy(weight_ref, scale_ref, load_sem.at[7])
    to_scalars.start()

    codes[...] = jnp.zeros_like(codes)
    codes[0, 0:6, :] = code_ref[pl.ds((row // 2) * 6, 6), :].astype(F32)
    lane_at = lax.broadcasted_iota(jnp.int32, (128, 128), 1)
    source_at = lax.broadcasted_iota(jnp.int32, (128, 128), 0)
    all_codes = code_ref[...].astype(F32)
    for k in range(6):
        n = lane_at + k * 128
        i = (n * 2731) >> 16
        place = (i * 16 + col) * SUB + (n - i * SUB)
        pick = (source_at == (place & 127)).astype(F32)
        lanes = dot(all_codes, pick, 1, 0, lax.Precision.HIGHEST)
        keep = source_at[0:96] == (place >> 7)[0:96]
        codes[1, k : k + 1, :] = jnp.sum(jnp.where(keep, lanes, 0.0), axis=0, keepdims=True)
    code = jnp.round(codes[...])
    order = jnp.floor(code * 0.5)
    quarter = (code - 2.0 * order) * 0.25

    @pl.loop(0, 16)
    def _(n4):
        for u in range(4):
            n = n4 * 4 + u
            angle = turns(order * n.astype(F32))
            trig_b[n, 0:2] = cos_turns(angle)
            trig_b[n, 2:4] = cos_turns(angle - 0.25)
            angle = turns(order * (n * 64).astype(F32)) - quarter
            trig_a[n, 0:2] = cos_turns(angle)
            trig_a[n, 2:4] = cos_turns(angle - 0.25)

    to_scalars.wait()

    def wave_part(first, last):
        @pl.loop(first // 128, last // 128)
        def _(n):
            for u in range(128):
                at = n * 128 + u
                l = lon_ref[at]
                a, b = l >> 6, l & 63
                rows = trig_a[a, 0] * trig_b[b, 0] - trig_a[a, 2] * trig_b[b, 2]
                wave[at, 0] = rows * scale_ref[n, u]
                wave[at, 1] = trig_a[a, 1] * trig_b[b, 1] - trig_a[a, 3] * trig_b[b, 3]

    def row_at(own_plane, off):
        return row_slot(c, p if own_plane else 1 - p, (y + off % 8) % 8)

    def col_at(own_plane, off):
        return col_slot((z + off % 8) % 8, h if own_plane else 1 - h, c)

    ways = ((row_at, along_y), (col_at, along_z))

    def take(slot, *onward):
        arrived(slot)
        for peer in onward:
            send(slot, peer)
        send(slot, sib)

    def second_stage(own_plane):
        for at, along in ways:
            onward = (along(2), along(1)) if own_plane else (along(1),)
            take(at(own_plane, -2), *onward)
        for at, along in ways:
            onward = (along(-1),) if own_plane else (along(-2), along(-1))
            take(at(own_plane, 2), *onward)

    def take_all(own_plane, offs):
        for off in offs:
            for at, _ in ways:
                take(at(own_plane, off))

    for at, along in ways:
        take(at(False, 0), along(2), along(-2), along(1), along(-1))
    wave_part(0, 512)
    second_stage(True)
    wave_part(512, 1792)
    second_stage(False)
    wave_part(1792, 2304)
    take_all(True, (1, -1))
    take_all(False, (1, -1))
    take_all(True, (3, -3, 4))
    wave_part(2304, 3072)
    take_all(False, (3, -3, 4))

    for copy in started[:40]:
        copy.wait_send()

    eye = (
        lax.broadcasted_iota(jnp.int32, (256, 256), 0)
        == lax.broadcasted_iota(jnp.int32, (256, 256), 1)
    ).astype(BF16)
    flat = table.reshape(2 * 1024 * 8, 128)

    def build(group):
        block = slots[pl.ds(group * 16, 16)].astype(F32)
        base = (group // 2) * (1024 * 8) + (group % 2) * 3
        for half in range(2):
            x = block[:, half * SUB : (half + 1) * SUB, :].reshape(TILE, 512).astype(BF16)
            for q in range(2):
                turned = dot(eye, x[:, q * 256 : (q + 1) * 256], 1, 1)
                for k in range(3):
                    first = base + (half * 512 + q * 256) * 8 + k
                    flat[pl.ds(first, 256, stride=8), :] = turned[:, k * 128 : (k + 1) * 128]

    build(c)

    @pl.loop(0, 16)
    def _(j):
        arrived((1 - c) * 16 + j)
        arrived(32 + j * 2 + (1 - c))

    @pl.loop(0, 3)
    def _(n):
        build(jnp.where(n == 0, 1 - c, n + 1))

    rhs_acc[...] = jnp.zeros_like(rhs_acc)

    def gather(blk):
        first = blk * BLOCK

        def some(b, acc):
            at = pl.multiple_of(b * (32 * 12), 8)
            for u in range(32):
                o = first + b * 32 + u
                t = colat_ref[o]
                scaled = table[0, t] * wave[o, 0]
                gathered[pl.ds(at + u * 12, 8), :] = scaled
                gathered[pl.ds(at + u * 12 + 6, 6), :] = (table[1, t] * wave[o, 1])[0:6]
                acc = acc + scaled * grad_ref[o]
            return acc

        rhs_acc[...] = lax.fori_loop(0, BLOCK // 32, some, rhs_acc[...])

    def left_of(half):
        first = ((1 - c) if half == 0 else c) * 3
        return jnp.concatenate(
            [gathered[pl.ds(first + k, BLOCK, stride=12), :].astype(BF16) for k in range(3)], axis=1
        )

    def right_of():
        return jnp.concatenate(
            [gathered[pl.ds(6 + k, BLOCK, stride=12), :].astype(BF16) for k in range(6)], axis=1
        )

    total[...] = jnp.zeros_like(total)

    @pl.loop(0, N_BLOCK - 1)
    def _(blk):
        gather(blk)
        left = jnp.concatenate([left_of(0), left_of(1)], axis=1)
        total[...] += dot(left, right_of(), 0, 0)

    last = N_BLOCK - 1
    gather(last)
    right = right_of()
    part[...] = (total[0:TILE, :] + dot(left_of(0), right, 0, 0)).astype(BF16)
    far = pltpu.make_async_remote_copy(
        src_ref=part, dst_ref=far_ref, send_sem=send_sem.at[N_SEND], recv_sem=far_sem.at[0],
        device_id=sib, device_id_type=MESH,
    )
    far.start()
    total[TILE : 2 * TILE, :] += dot(left_of(1), right, 0, 0)
    near_copy = pltpu.make_async_copy(total.at[pl.ds(TILE, TILE)], own_ref, load_sem.at[0])
    near_copy.start()
    rhs_part[...] = jnp.zeros_like(rhs_part)
    rhs_ref[...] = jnp.zeros_like(rhs_ref)
    rhs_part[0:3, :] = rhs_acc[pl.ds((1 - c) * 3, 3), :]
    rhs_ref[0:3, :] = rhs_acc[pl.ds(c * 3, 3), :]
    far_rhs = pltpu.make_async_remote_copy(
        src_ref=rhs_part, dst_ref=far_rhs_ref, send_sem=send_sem.at[N_SEND + 1],
        recv_sem=far_sem.at[1], device_id=sib, device_id_type=MESH,
    )
    far_rhs.start()
    for copy in started[40:]:
        copy.wait_send()
    near_copy.wait()
    far_rhs.wait()
    far.wait()


def finish(own_ref, rhs_ref, far_ref, far_rhs_ref, normal_ref, sum_ref):
    normal_ref[0] = (own_ref[...] + far_ref[...].astype(F32)) * (1.0 / OBS)

    @pl.when(pl.program_id(0) == 0)
    def _():
        sum_ref[...] = ((rhs_ref[0:3, :] + far_rhs_ref[0:3, :]) * (1.0 / OBS)).reshape(TILE)


def shards(leg_table, coef_code, colat_idx, lon_idx, gap_mask, obs_weight, gradient):
    vmem = pl.BlockSpec(memory_space=pltpu.VMEM)
    hbm = pl.BlockSpec(memory_space=pl.ANY)
    own, own_rhs, far, far_rhs = pl.pallas_call(
        kernel,
        out_shape=(
            jax.ShapeDtypeStruct((TILE, 768), F32),
            jax.ShapeDtypeStruct((8, 128), F32),
            jax.ShapeDtypeStruct((TILE, 768), BF16),
            jax.ShapeDtypeStruct((8, 128), F32),
        ),
        in_specs=[hbm] * 7,
        out_specs=(hbm, vmem, hbm, hbm),
        scratch_shapes=[
            pltpu.VMEM((64, 2 * SUB, 512), BF16),
            pltpu.VMEM((SUB, NTHETA), BF16),
            pltpu.VMEM((SUB, 1024), F32),
            pltpu.VMEM((2, 1024, 8, 128), F32),
            pltpu.VMEM((HALF, 2, 8, 128), F32),
            pltpu.VMEM((64, 4, 8, 128), F32),
            pltpu.VMEM((64, 4, 8, 128), F32),
            pltpu.VMEM((2, 8, 128), F32),
            pltpu.VMEM((BLOCK * 12, 128), F32),
            pltpu.VMEM((768, 768), F32),
            pltpu.VMEM((TILE, 768), BF16),
            pltpu.VMEM((8, 128), F32),
            pltpu.VMEM((8, 128), F32),
            pltpu.VMEM((96, 128), jnp.int32),
            pltpu.VMEM((HALF // 128, 128), jnp.int32),
            pltpu.VMEM((HALF // 128, 128), F32),
            pltpu.SMEM((HALF // 128, 128), F32),
            pltpu.SMEM((HALF,), F32),
            pltpu.SMEM((HALF,), jnp.int32),
            pltpu.SMEM((HALF,), jnp.int32),
            pltpu.SemaphoreType.DMA((N_SEND + 2,)),
            pltpu.SemaphoreType.DMA((64,)),
            pltpu.SemaphoreType.DMA((2,)),
            pltpu.SemaphoreType.DMA((8,)),
        ],
        compiler_params=pltpu.CompilerParams(
            collective_id=0, has_side_effects=True, vmem_limit_bytes=62 * 2**20
        ),
    )(
        leg_table.T, coef_code.reshape(96, 128), gap_mask.reshape(48, 128),
        obs_weight.reshape(48, 128), gradient, colat_idx, lon_idx,
    )
    half = TILE // 2
    normal, rhs = pl.pallas_call(
        finish,
        grid=(2,),
        in_specs=[
            pl.BlockSpec((half, 768), lambda i: (i, 0)),
            pl.BlockSpec((8, 128), lambda i: (0, 0)),
            pl.BlockSpec((half, 768), lambda i: (i, 0)),
            pl.BlockSpec((8, 128), lambda i: (0, 0)),
        ],
        out_specs=(
            pl.BlockSpec((1, half, 768), lambda i: (0, i, 0)),
            pl.BlockSpec((TILE,), lambda i: (0,)),
        ),
        out_shape=(
            jax.ShapeDtypeStruct((1, TILE, 768), F32),
            jax.ShapeDtypeStruct((TILE,), F32),
        ),
    )(own, own_rhs, far, far_rhs)
    return normal, rhs


def solution(mesh):
    placed = (P(None, ("row", "col")), P(), P(), P(), P(), P(), P())
    return jax.shard_map(
        shards,
        mesh=mesh,
        in_specs=placed,
        out_specs=(P("col", "row", None), P("row")),
        check_vma=False,
    )
```

```python
import functools

import jax
import jax.numpy as jnp
from jax import lax
from jax.experimental import pallas as pl
from jax.experimental.pallas import tpu as pltpu
from jax.sharding import PartitionSpec as P

NLON = 3600
NTHETA = 900
OBS = 6144
SUB = 24
HALF = OBS // 2
BLOCK = 1024
N_BLOCK = HALF // BLOCK
TILE = 384
F32 = jnp.float32
BF16 = jnp.bfloat16
MESH = pl.DeviceIdType.MESH
N_SEND = 62


def sin_turns(w):
    s = w * w
    p = -76.58128455924857 + s * 39.76072207493176
    p = 81.60248074286099 + s * p
    p = -41.341680668063056 + s * p
    p = 6.283185280261415 + s * p
    return w * p


def cos_turns(f):
    return sin_turns(0.25 - jnp.abs(f - jnp.round(f)))


def turns(x):
    return (x - NLON * jnp.round(x * (1.0 / NLON))) * (1.0 / NLON)


def dot(a, b, ca, cb, precision=None):
    return lax.dot_general(
        a, b, (((ca,), (cb,)), ((), ())), preferred_element_type=F32, precision=precision
    )


def kernel(
    leg_hbm, code_hbm, mask_hbm, weight_hbm, grad_hbm, colat_hbm, lon_hbm,
    own_ref, rhs_ref, far_ref, far_rhs_ref,
    slots, leg_ref, fold, table, wave, trig_a, trig_b, codes, gathered,
    total, part, rhs_acc, rhs_part, code_ref, mask_ref, weight_ref, scale_ref, grad_ref, colat_ref, lon_ref,
    send_sem, slot_sem, far_sem, load_sem,
):
    row, col = lax.axis_index("row"), lax.axis_index("col")
    z, h, c = row // 4, (row // 2) % 2, row % 2
    p, y = col // 8, col % 8

    def rid(z_, h_, c_):
        return z_ * 4 + h_ * 2 + c_

    def cid(p_, y_):
        return p_ * 8 + y_

    sib = (rid(z, h, 1 - c), col)
    over_p = (row, cid(1 - p, y))
    over_h = (rid(z, 1 - h, c), col)

    def along_y(off):
        return (row, cid(p, (y + off % 8) % 8))

    def along_z(off):
        return (rid((z + off % 8) % 8, h, c), col)

    near = (1, 2, -1, -2)
    peers = (sib, over_p, over_h) + tuple(along_y(o) for o in near) + tuple(along_z(o) for o in near)

    barrier = pltpu.get_barrier_semaphore()
    for peer in peers:
        pl.semaphore_signal(barrier, inc=1, device_id=peer, device_id_type=MESH)

    my_half = pl.ds(pl.multiple_of(c * HALF, HALF), HALF)
    my_rows = pl.ds(pl.multiple_of(c * (HALF // 128), 8), HALF // 128)
    loads = [
        pltpu.make_async_copy(src, dst, load_sem.at[n])
        for n, (src, dst) in enumerate((
            (leg_hbm, leg_ref), (code_hbm, code_ref.at[pl.ds(0, 96)]), (lon_hbm.at[my_half], lon_ref),
            (colat_hbm.at[my_half], colat_ref), (weight_hbm.at[my_rows], weight_ref),
            (mask_hbm.at[my_rows], mask_ref), (grad_hbm.at[my_half], grad_ref),
        ))
    ]
    for load in loads:
        load.start()

    def row_slot(core, plane, y_):
        return core * 16 + plane * 8 + y_

    def col_slot(z_, plane, core):
        return 32 + z_ * 4 + plane * 2 + core

    fold[...] = jnp.zeros_like(fold)
    loads[0].wait()
    fold[:, 0:NTHETA] = leg_ref[...].astype(F32)
    own = jnp.concatenate([fold[:, 0:512], fold[:, 512:1024]], axis=0).astype(BF16)
    mine_r, mine_c = row_slot(c, p, y), col_slot(z, h, c)
    slots[mine_r] = own
    slots[mine_c] = own

    started = []

    def copy_of(slot, peer, sem_at):
        return pltpu.make_async_remote_copy(
            src_ref=slots.at[slot], dst_ref=slots.at[slot],
            send_sem=send_sem.at[sem_at], recv_sem=slot_sem.at[slot],
            device_id=peer, device_id_type=MESH,
        )

    def send(slot, peer):
        copy = copy_of(slot, peer, len(started))
        copy.start()
        started.append(copy)

    def arrived(slot):
        copy_of(slot, sib, 0).wait_recv()

    pl.semaphore_wait(barrier, len(peers))

    for off in (2, -2):
        send(mine_r, along_y(off))
        send(mine_c, along_z(off))
    send(mine_r, over_p)
    send(mine_c, over_h)
    for off in (1, -1):
        send(mine_r, along_y(off))
        send(mine_c, along_z(off))
    send(mine_r, sib)
    send(mine_c, sib)
    for load in loads[1:]:
        load.wait()
    weight_ref[...] = weight_ref[...] * mask_ref[...].astype(F32)
    to_scalars = pltpu.make_async_copy(weight_ref, scale_ref, load_sem.at[7])
    to_scalars.start()

    codes[...] = jnp.zeros_like(codes)
    codes[0, 0:6, :] = code_ref[pl.ds((row // 2) * 6, 6), :].astype(F32)
    lane_at = lax.broadcasted_iota(jnp.int32, (128, 128), 1)
    source_at = lax.broadcasted_iota(jnp.int32, (128, 128), 0)
    all_codes = code_ref[0:96, :].astype(F32)
    for k in range(6):
        n = lane_at + k * 128
        i = (n * 2731) >> 16
        place = (i * 16 + col) * SUB + (n - i * SUB)
        pick = (source_at == (place & 127)).astype(F32)
        lanes = dot(all_codes, pick, 1, 0, lax.Precision.HIGHEST)
        keep = source_at[0:96] == (place >> 7)[0:96]
        codes[1, k : k + 1, :] = jnp.sum(jnp.where(keep, lanes, 0.0), axis=0, keepdims=True)
    code = jnp.round(codes[...])
    order = jnp.floor(code * 0.5)
    quarter = (code - 2.0 * order) * 0.25

    @pl.loop(0, 16)
    def _(n4):
        for u in range(4):
            n = n4 * 4 + u
            angle = turns(order * n.astype(F32))
            trig_b[n, 0:2] = cos_turns(angle)
            trig_b[n, 2:4] = cos_turns(angle - 0.25)
            angle = turns(order * (n * 64).astype(F32)) - quarter
            trig_a[n, 0:2] = cos_turns(angle)
            trig_a[n, 2:4] = cos_turns(angle - 0.25)

    to_scalars.wait()

    def wave_part(first, last):
        @pl.loop(first // 128, last // 128)
        def _(n):
            for u in range(128):
                at = n * 128 + u
                l = lon_ref[at]
                a, b = l >> 6, l & 63
                rows = trig_a[a, 0] * trig_b[b, 0] - trig_a[a, 2] * trig_b[b, 2]
                wave[at, 0] = rows * scale_ref[n, u]
                wave[at, 1] = trig_a[a, 1] * trig_b[b, 1] - trig_a[a, 3] * trig_b[b, 3]

    def row_at(own_plane, off):
        return row_slot(c, p if own_plane else 1 - p, (y + off % 8) % 8)

    def col_at(own_plane, off):
        return col_slot((z + off % 8) % 8, h if own_plane else 1 - h, c)

    ways = ((row_at, along_y), (col_at, along_z))

    def take(slot, *onward):
        arrived(slot)
        for peer in onward:
            send(slot, peer)
        send(slot, sib)

    def second_stage(own_plane):
        for at, along in ways:
            onward = (along(2), along(1)) if own_plane else (along(1),)
            take(at(own_plane, -2), *onward)
        for at, along in ways:
            onward = (along(-1),) if own_plane else (along(-2), along(-1))
            take(at(own_plane, 2), *onward)

    def take_all(own_plane, offs):
        for off in offs:
            for at, _ in ways:
                take(at(own_plane, off))

    for at, along in ways:
        take(at(False, 0), along(2), along(-2), along(1), along(-1))
    wave_part(0, 512)
    second_stage(True)
    wave_part(512, 1792)
    second_stage(False)
    wave_part(1792, 2304)
    take_all(True, (1, -1))
    take_all(False, (1, -1))
    take_all(True, (3, -3, 4))
    wave_part(2304, 3072)
    take_all(False, (3, -3, 4))

    for copy in started[:40]:
        copy.wait_send()

    eye = (
        lax.broadcasted_iota(jnp.int32, (256, 256), 0)
        == lax.broadcasted_iota(jnp.int32, (256, 256), 1)
    ).astype(BF16)
    flat = table.reshape(2 * 1024 * 8, 128)

    def build(group):
        block = slots[pl.ds(group * 16, 16)].astype(F32)
        base = (group // 2) * (1024 * 8) + (group % 2) * 3
        for half in range(2):
            x = block[:, half * SUB : (half + 1) * SUB, :].reshape(TILE, 512).astype(BF16)
            for q in range(2):
                turned = dot(eye, x[:, q * 256 : (q + 1) * 256], 1, 1)
                for k in range(3):
                    first = base + (half * 512 + q * 256) * 8 + k
                    flat[pl.ds(first, 256, stride=8), :] = turned[:, k * 128 : (k + 1) * 128]

    build(c)

    @pl.loop(0, 16)
    def _(j):
        arrived((1 - c) * 16 + j)
        arrived(32 + j * 2 + (1 - c))

    @pl.loop(0, 3)
    def _(n):
        build(jnp.where(n == 0, 1 - c, n + 1))

    rhs_acc[...] = jnp.zeros_like(rhs_acc)

    def gather(blk):
        first = blk * BLOCK

        def some(b, acc):
            at = pl.multiple_of(b * (32 * 12), 8)
            for u in range(32):
                o = first + b * 32 + u
                t = colat_ref[o]
                scaled = table[0, t] * wave[o, 0]
                gathered[pl.ds(at + u * 12, 8), :] = scaled
                gathered[pl.ds(at + u * 12 + 6, 6), :] = (table[1, t] * wave[o, 1])[0:6]
                acc = acc + scaled * grad_ref[o]
            return acc

        rhs_acc[0:8, :] = lax.fori_loop(0, BLOCK // 32, some, rhs_acc[0:8, :])

    def left_of(half):
        first = ((1 - c) if half == 0 else c) * 3
        return jnp.concatenate(
            [gathered[pl.ds(first + k, BLOCK, stride=12), :].astype(BF16) for k in range(3)], axis=1
        )

    def right_of():
        return jnp.concatenate(
            [gathered[pl.ds(6 + k, BLOCK, stride=12), :].astype(BF16) for k in range(6)], axis=1
        )

    total[...] = jnp.zeros_like(total)

    @pl.loop(0, N_BLOCK - 1)
    def _(blk):
        gather(blk)
        left = jnp.concatenate([left_of(0), left_of(1)], axis=1)
        total[...] += dot(left, right_of(), 0, 0)

    last = N_BLOCK - 1
    gather(last)
    right = right_of()
    part[...] = (total[0:TILE, :] + dot(left_of(0), right, 0, 0)).astype(BF16)
    far = pltpu.make_async_remote_copy(
        src_ref=part, dst_ref=far_ref, send_sem=send_sem.at[N_SEND], recv_sem=far_sem.at[0],
        device_id=sib, device_id_type=MESH,
    )
    far.start()
    total[TILE : 2 * TILE, :] += dot(left_of(1), right, 0, 0)
    near_copy = pltpu.make_async_copy(total.at[pl.ds(TILE, TILE)], own_ref, load_sem.at[0])
    near_copy.start()
    rhs_part[...] = jnp.zeros_like(rhs_part)
    rhs_ref[...] = jnp.zeros_like(rhs_ref)
    rhs_part[0:3, :] = rhs_acc[pl.ds((1 - c) * 3, 3), :]
    rhs_ref[0:3, :] = rhs_acc[pl.ds(c * 3, 3), :]
    far_rhs = pltpu.make_async_remote_copy(
        src_ref=rhs_part, dst_ref=far_rhs_ref, send_sem=send_sem.at[N_SEND + 1],
        recv_sem=far_sem.at[1], device_id=sib, device_id_type=MESH,
    )
    far_rhs.start()
    for copy in started[40:]:
        copy.wait_send()
    near_copy.wait()
    far_rhs.wait()
    far.wait()


def finish(own_ref, rhs_ref, far_ref, far_rhs_ref, normal_ref, sum_ref):
    normal_ref[0] = (own_ref[...] + far_ref[...].astype(F32)) * (1.0 / OBS)

    @pl.when(pl.program_id(0) == 0)
    def _():
        sum_ref[...] = ((rhs_ref[0:3, :] + far_rhs_ref[0:3, :]) * (1.0 / OBS)).reshape(TILE)


def shards(leg_table, coef_code, colat_idx, lon_idx, gap_mask, obs_weight, gradient):
    vmem = pl.BlockSpec(memory_space=pltpu.VMEM)
    hbm = pl.BlockSpec(memory_space=pl.ANY)
    own, own_rhs, far, far_rhs = pl.pallas_call(
        kernel,
        out_shape=(
            jax.ShapeDtypeStruct((TILE, 768), F32),
            jax.ShapeDtypeStruct((8, 128), F32),
            jax.ShapeDtypeStruct((TILE, 768), BF16),
            jax.ShapeDtypeStruct((8, 128), F32),
        ),
        in_specs=[hbm] * 7,
        out_specs=(hbm, vmem, hbm, hbm),
        scratch_shapes=[
            pltpu.VMEM((64, 2 * SUB, 512), BF16),
            pltpu.VMEM((SUB, NTHETA), BF16),
            pltpu.VMEM((SUB, 1024), F32),
            pltpu.VMEM((2, 1024, 8, 128), F32),
            pltpu.VMEM((HALF, 2, 8, 128), F32),
            pltpu.VMEM((64, 4, 8, 128), F32),
            pltpu.VMEM((64, 4, 8, 128), F32),
            pltpu.VMEM((2, 8, 128), F32),
            pltpu.VMEM((BLOCK * 12 + 8, 128), F32),
            pltpu.VMEM((768, 768), F32),
            pltpu.VMEM((TILE, 768), BF16),
            pltpu.VMEM((16, 128), F32),
            pltpu.VMEM((8, 128), F32),
            pltpu.VMEM((104, 128), jnp.int32),
            pltpu.VMEM((HALF // 128, 128), jnp.int32),
            pltpu.VMEM((HALF // 128, 128), F32),
            pltpu.SMEM((HALF // 128, 128), F32),
            pltpu.SMEM((HALF,), F32),
            pltpu.SMEM((HALF,), jnp.int32),
            pltpu.SMEM((HALF,), jnp.int32),
            pltpu.SemaphoreType.DMA((N_SEND + 2,)),
            pltpu.SemaphoreType.DMA((64,)),
            pltpu.SemaphoreType.DMA((2,)),
            pltpu.SemaphoreType.DMA((8,)),
        ],
        compiler_params=pltpu.CompilerParams(
            collective_id=0, has_side_effects=True, vmem_limit_bytes=62 * 2**20
        ),
    )(
        leg_table.T, coef_code.reshape(96, 128), gap_mask.reshape(48, 128),
        obs_weight.reshape(48, 128), gradient, colat_idx, lon_idx,
    )
    half = TILE // 2
    normal, rhs = pl.pallas_call(
        finish,
        grid=(2,),
        in_specs=[
            pl.BlockSpec((half, 768), lambda i: (i, 0)),
            pl.BlockSpec((8, 128), lambda i: (0, 0)),
            pl.BlockSpec((half, 768), lambda i: (i, 0)),
            pl.BlockSpec((8, 128), lambda i: (0, 0)),
        ],
        out_specs=(
            pl.BlockSpec((1, half, 768), lambda i: (0, i, 0)),
            pl.BlockSpec((TILE,), lambda i: (0,)),
        ),
        out_shape=(
            jax.ShapeDtypeStruct((1, TILE, 768), F32),
            jax.ShapeDtypeStruct((TILE,), F32),
        ),
    )(own, own_rhs, far, far_rhs)
    return normal, rhs


def solution(mesh):
    placed = (P(None, ("row", "col")), P(), P(), P(), P(), P(), P())
    return jax.shard_map(
        shards,
        mesh=mesh,
        in_specs=placed,
        out_specs=(P("col", "row", None), P("row")),
        check_vma=False,
    )
```
